1024 devices in a mesh: dp: 16 (over z), ctx: 16 (over y_lo, x, core), tp: 4 (over y_hi).
Axes of the slice: x: 4, y: 8 (y_hi: 4, y_lo: 2; y = y_hi * 2 + y_lo), z: 16, core: 2. Of those that a mesh axis runs over, the one named last changes fastest.
Arguments:
- hidden: bfloat16 [393216, 768], P(('dp', 'ctx', 'tp')), may hold values from -24 to 24
- grad_output: bfloat16 [131072, 2048], P(('dp', 'ctx', 'tp')), may hold values from -6 to 6
- expert_ids: int32 [131072, 2], P(('dp', 'ctx', 'tp')), may hold values from 0 to 63, all different within a row; in each aligned block of 128 rows (0 to 127, 128 to 255, ...) at most 6 rows name the same one
- gate_weights: float32 [131072, 2], P(('dp', 'ctx', 'tp')), may hold values from 0.2 to 1
- w_down: bfloat16 [64, 768, 2048], P(('ctx', 'tp')), may hold values from -0.21875 to 0.21875
Outputs:
- combined: bfloat16 [131072, 2048], P(('dp', 'ctx', 'tp'))
- grad_hidden: bfloat16 [393216, 768], P(('dp', 'ctx', 'tp'))
- grad_down: bfloat16 [64, 768, 2048], P(('ctx', 'tp'), 'dp')
The draws below stay inside these ranges and needn't reach their ends.
Inputs may be any that keep to these rules, and one draw needn't show every extreme that they name: `expert_ids`: each row names 2 different experts. Among the 128 rows of one device no expert is named more than 6 times, and in every draw some device names some expert exactly 6 times.
All inputs are finite; a program needn't handle non-finite values.
Results may differ from the reference program's by a relative error of at most 0.017.
Values may be sent and summed in bfloat16 or wider, within the bound.
A program may use at most 64 MiB of HBM per device.

```python
import math
import jax
import jax.numpy as jnp
import numpy as np
from jax import lax

D = 2048
FF = 768
TOPK = 2
TOK_DEV = 128
EXPERTS = 64
CAP = 6
TOKENS = 131072
N_DP = 16
DEVICES = 1024


def raised(drawn, stream_key, source, target, parts, factor):
    owner, partner = [(jnp.arange(drawn.shape[axis_at]) // (drawn.shape[axis_at] // parts)).reshape([-1 if axis == axis_at else 1 for axis in range(drawn.ndim)]) for axis_at in (source, target)]
    chosen = jax.random.permutation(stream_key, parts)[partner]
    strong = (owner == chosen) | (owner == (partner + parts // 2) % parts)
    return jnp.where(strong, factor * drawn, drawn)


def level_of(own_key, dims, cuts, low, largest):
    level, own = 1.0, jax.random.fold_in(own_key, 6)
    for position, blocks in cuts:
        draws = jnp.exp(jax.random.uniform(jax.random.fold_in(own, position), (blocks,), jnp.float32, low / len(cuts), largest / len(cuts)))
        level = level * jnp.repeat(draws, dims[position] // blocks).reshape([-1 if axis == position else 1 for axis in range(len(dims))])
    return level


def shared_out(stream_key, own, number, rows, count, top, limit, lean):
    order = jax.random.permutation(stream_key, count)
    heavy_load, common = portions_of(count, rows * top, limit, lean, True), portions_of(count, rows * top, limit, lean, False)
    places = jnp.arange(count)

    def named(sizes, turn):
        used = int((sizes > 0).sum())
        fixed = max(1, used // 4)
        shifted = fixed + (places - fixed + turn * (used - fixed)) % max(1, count - fixed)
        return jnp.zeros((count,), jnp.int32).at[order[jnp.where(places < fixed, places, shifted)]].set(jnp.asarray(sizes, jnp.int32))

    sizes = jnp.where(number % 4 == 0, named(heavy_load, number // 4), named(common, number - number // 4 - 1))
    mixed = jax.random.permutation(jax.random.fold_in(own, 3), count)
    source_of, taker = mixed[0:count // 2 * 2:2], mixed[1:count // 2 * 2:2]
    margin = jnp.minimum(sizes[source_of] - 1, limit - sizes[taker]) // 2
    margin = jnp.where((source_of == order[0]) | (taker == order[0]) | (sizes[taker] == 0), 0, jnp.maximum(margin, 0))
    shifted = jax.random.randint(jax.random.fold_in(own, 4), (count // 2,), 0, 1 << 20) % (margin + 1)
    sizes = sizes.at[source_of].add(-shifted).at[taker].add(shifted)
    members = jnp.searchsorted(jnp.cumsum(sizes), jnp.arange(rows * top), side="right").astype(jnp.int32)
    table = members.reshape(top, rows).T
    table = table[jax.random.permutation(jax.random.fold_in(own, 1), rows)]
    turn = jax.random.randint(jax.random.fold_in(own, 2), (rows, 1), 0, top)
    return jnp.take_along_axis(table, (jnp.arange(top)[None, :] + turn) % top, axis=1)


def portions_of(number_of, total, bound, lean, full):
    loads = [(1 << 20) // math.isqrt(grade ** lean) + 1 for grade in range(1, number_of + 1)]
    largest = bound if full else min(bound, max(-(-total // number_of), total * loads[0] // sum(loads)))
    least = 1 if total - largest >= number_of - 1 else 0
    given, rest = [largest] + [least] * (number_of - 1), total - largest - least * (number_of - 1)
    while rest > 0:
        movable = [i for i in range(1, number_of) if given[i] < largest] or [i for i in range(1, number_of) if given[i] < bound]
        pool, budget = sum([loads[i] for i in movable]), rest
        for i in movable:
            extra = min(bound - given[i], max(1, budget * loads[i] // pool), rest)
            given[i] = given[i] + extra
            rest = rest - extra
    return np.array(given)


def normal_values(stream_key, shape, width, reach, cuts=(), kind=jnp.bfloat16):
    factor_of = level_of(stream_key, shape, cuts, -0.22, 0.18) if cuts else 1.0
    values = jax.random.normal(stream_key, shape, jnp.float32) * width * factor_of
    return jnp.minimum(jnp.maximum(values, -reach), reach).astype(kind)


def heavy_noise(key, extent, deviation, bound, cuts, heavy, kind=jnp.bfloat16):
    result = deviation * jax.random.normal(key, extent, jnp.float32)
    if cuts:
        result = result * level_of(key, extent, cuts, -0.22, 0.18)
    return jnp.clip(raised(result, jax.random.fold_in(key, 3), *heavy), -bound, bound).astype(kind)


def setup_inputs(seed: int = 0) -> dict:
    keys = jax.random.split(jax.random.key(seed), 6)
    hidden = heavy_noise(keys[0], (DEVICES * EXPERTS * CAP, FF), 1.0, 24.0, ((0, 1024),), (0, 1, 256, 6.0))
    grad_output = normal_values(keys[1], (TOKENS, D), 1.0, 6.0, ((0, 1024),))
    expert_ids_keys = jax.random.split(jax.random.fold_in(keys[2], 1), TOKENS // TOK_DEV)
    expert_ids_turns = jax.random.permutation(jax.random.fold_in(keys[2], 3), TOKENS // TOK_DEV)
    expert_ids = jax.vmap(lambda own, number: shared_out(jax.random.fold_in(keys[2], 2), own, number, TOK_DEV, EXPERTS, TOPK, CAP, 2))(expert_ids_keys, expert_ids_turns).reshape((TOKENS, TOPK))
    gate_weights = jnp.clip(0.2 + 0.8 * jax.random.uniform(keys[3], (TOKENS, TOPK), jnp.float32) ** level_of(keys[3], (TOKENS, TOPK), ((0, 1024),), -0.2, 0.2), 0.2, 1.0)
    w_down = normal_values(keys[4], (EXPERTS, FF, D), FF ** -0.5, 0.21875, ((0, 64),))
    return {"hidden": hidden, "grad_output": grad_output, "expert_ids": expert_ids, "gate_weights": gate_weights, "w_down": w_down}


grad_scale = 0.015625


def slot_index(ids_block):
    flat_ids = ids_block.reshape(-1).astype(jnp.int32)
    one_hot = (flat_ids[:, None] == jnp.arange(EXPERTS, dtype=jnp.int32)[None, :]).astype(jnp.int32)
    earlier = jnp.cumsum(one_hot, axis=0) - one_hot
    ranking = jnp.sum(earlier * one_hot, axis=1)
    return (flat_ids * CAP + ranking).astype(jnp.int32)


def expert_forward(operands):
    rows, matrix = operands
    return jnp.dot(rows, matrix, preferred_element_type=jnp.float32).astype(jnp.bfloat16)


def expert_backward(operands):
    rows, matrix, grads = operands
    grad_rows = lax.dot_general(grads, matrix, (((1,), (1,)), ((), ())), preferred_element_type=jnp.float32).astype(jnp.bfloat16)
    weight_part = lax.dot_general(rows, grads, (((0,), (0,)), ((), ())), preferred_element_type=jnp.float32)
    weight_part = lax.optimization_barrier(weight_part.astype(jnp.bfloat16)).astype(jnp.float32)
    return grad_rows, weight_part


def take_rows(table, positions):
    return table[positions]


def place_rows(positions, values):
    return jnp.zeros((EXPERTS * CAP, D), values.dtype).at[positions].set(values)


def make_group(w_down):
    def per_group(summed, inputs):
        hidden_group, grad_group, ids_group, gate_group = inputs
        positions = jax.vmap(slot_index)(ids_group)
        expert_out = lax.map(expert_forward, (hidden_group, w_down))
        by_source = expert_out.reshape(EXPERTS, EXPERTS, CAP, D).transpose(1, 0, 2, 3).reshape(EXPERTS, EXPERTS * CAP, D)
        picked = jax.vmap(take_rows)(by_source, positions).astype(jnp.float32).reshape(EXPERTS, TOK_DEV, TOPK, D)
        combined = jnp.sum(gate_group[..., None] * picked, axis=2).astype(jnp.bfloat16)
        scaled = (gate_group[..., None] * grad_group[:, :, None, :].astype(jnp.float32)).astype(jnp.bfloat16)
        scaled = scaled.reshape(EXPERTS, TOK_DEV * TOPK, D)
        outgoing = jax.vmap(place_rows)(positions, scaled)
        incoming = outgoing.reshape(EXPERTS, EXPERTS, CAP, D).transpose(1, 0, 2, 3).reshape(EXPERTS, EXPERTS * CAP, D)
        grad_rows, weight_part = lax.map(expert_backward, (hidden_group, w_down, incoming))
        return summed + weight_part, (combined, grad_rows)
    return per_group


def reference(hidden, grad_output, expert_ids, gate_weights, w_down):
    hidden_groups = hidden.reshape(N_DP, EXPERTS, EXPERTS * CAP, FF)
    grad_groups = grad_output.reshape(N_DP, EXPERTS, TOK_DEV, D)
    id_groups = expert_ids.reshape(N_DP, EXPERTS, TOK_DEV, TOPK)
    gate_groups = gate_weights.reshape(N_DP, EXPERTS, TOK_DEV, TOPK)
    zero_sum = jnp.zeros((EXPERTS, FF, D), jnp.float32)
    summed, (combined, grad_rows) = lax.scan(make_group(w_down), zero_sum, (hidden_groups, grad_groups, id_groups, gate_groups))
    grad_down = (summed * grad_scale).astype(jnp.bfloat16)
    return combined.reshape(grad_output.shape), grad_rows.reshape(hidden.shape), grad_down
```

```python
import functools

import jax
import jax.numpy as jnp
from jax import lax
from jax.experimental import pallas as pl
from jax.experimental.pallas import tpu as pltpu
from jax.sharding import PartitionSpec as P

MESH = pl.DeviceIdType.MESH
GRAD_SCALE = 0.015625
F32, BF16 = jnp.float32, jnp.bfloat16

NY, NX, NC, NZ = 8, 4, 2, 16
CAP = 6
GROUP = 8 * CAP
ROWS = 64 * CAP
CHUNKS = 4
HUB, PLANE_MEMBER, Z_MEMBER = 4, 0, 2


def events(chunks):
    tick = 34.0 / chunks
    out = []
    for k in range(chunks):
        out.append((0.0 + 0.01 * k, "send_y", k, 0))
        arrive_y = 4.0 + tick * (k + 1)
        out.append((arrive_y, "send_x", k, 0))
        arrive_x = arrive_y + 2.0 + tick * 0.55
        out.append((arrive_x, "part", k, 0))
        for j in range(1, 9):
            out.append((arrive_x + 2.6 * j, "ring", k, j))
        out.append((1.0 + tick * k * 0.8, "back_x", k, 0))
        out.append((4.0 + tick * (chunks - 1.1 + k), "back_y", k, 0))
        out.append((7.0 + tick * (chunks + 1 + k), "combine", k, 0))
    return sorted(out)


def kernel(
    ids_ref, gate_ref, hid_hbm, grad_hbm, w_hbm,
    comb_hbm, gh_hbm, gd_hbm,
    hid, grad, w, hp, hpt, perm, unsort, slot_pick, pick0, pick1, slot_gate, tok_gate,
    y_out, y_in, x_out, x_in, part, ring_up, ring_dn,
    ex, bx_in, by_out, by_in, gh_acc, comb, gh, gd,
    in_sem, out_sem, ring_ok, plane_ok, z_ok,
    y_s, y_r, x_s, x_r, bx_s, bx_r, by_s, by_r, up_s, up_r, dn_s, dn_r,
):
    tok = grad.shape[0]
    width = y_in.shape[2]
    z = lax.axis_index("dp")
    ctx = lax.axis_index("ctx")
    tp = lax.axis_index("tp")
    c = lax.rem(ctx, 2)
    x = lax.rem(ctx // 2, 4)
    y = tp * 2 + ctx // 8

    def dev(dz=0, dy=0, dx=0, dc=0):
        ny = lax.rem(y + (dy + NY), NY)
        nx = lax.rem(x + (dx + NX), NX)
        nc = lax.rem(c + (dc + NC), NC)
        nz = lax.rem(z + (dz + NZ), NZ)
        return {"dp": nz, "ctx": (lax.rem(ny, 2) * NX + nx) * NC + nc, "tp": ny // 2}

    loads = [
        pltpu.make_async_copy(grad_hbm, grad, in_sem.at[0]),
        pltpu.make_async_copy(hid_hbm, hid, in_sem.at[1]),
        pltpu.make_async_copy(w_hbm.at[0], w, in_sem.at[2]),
    ]
    for cp in loads:
        cp.start()

    barrier = pltpu.get_barrier_semaphore()

    def tell_ring(sem):
        for d in range(1, NY):
            pl.semaphore_signal(sem, inc=1, device_id=dev(dy=d), device_id_type=MESH)

    @pl.when(y != HUB)
    def _():
        pl.semaphore_signal(barrier, inc=1, device_id=dev(dy=HUB - y + NY), device_id_type=MESH)

    def greet_ring():
        @pl.when(y == HUB)
        def _():
            pl.semaphore_wait(barrier, NY - 1)
            tell_ring(ring_ok)

        @pl.when(y != HUB)
        def _():
            pl.semaphore_wait(ring_ok, 1)

        @pl.when(y == PLANE_MEMBER)
        def _():
            for d in range(1, 8):
                pl.semaphore_signal(barrier, inc=1, device_id=dev(dx=d // 2, dc=d % 2), device_id_type=MESH)

        @pl.when(y == Z_MEMBER)
        def _():
            for d in (1, -1):
                pl.semaphore_signal(barrier, inc=1, device_id=dev(dz=d), device_id_type=MESH)

    def greet_others(member, count, sem):
        @pl.when(y == member)
        def _():
            pl.semaphore_wait(barrier, count)
            tell_ring(sem)

        @pl.when(y != member)
        def _():
            pl.semaphore_wait(sem, 1)

    def send(src, dst, ssem, rsem, device):
        return pltpu.make_async_remote_copy(
            src_ref=src, dst_ref=dst, send_sem=ssem, recv_sem=rsem, device_id=device, device_id_type=MESH
        )

    def group(d):
        return pl.ds(d * GROUP, GROUP)

    def y_copy(k, d):
        return send(y_out.at[k, group(d)], y_in.at[k, group(d)], y_s.at[k, d], y_r.at[k, d], dev(dy=d))

    def x_copy(k, d):
        return send(
            x_out.at[k, group(d)], x_in.at[k, group(d)], x_s.at[k, d], x_r.at[k, d], dev(dx=d // 2, dc=d % 2)
        )

    def bx_copy(k, d):
        return send(
            ex.at[k, group(d)], bx_in.at[k, group(d)], bx_s.at[k, d], bx_r.at[k, d], dev(dx=-(d // 2), dc=d % 2)
        )

    def by_copy(k, d):
        return send(by_out.at[k, group(d)], by_in.at[k, group(d)], by_s.at[k, d], by_r.at[k, d], dev(dy=-d))

    def block(b):
        return pl.ds(pl.multiple_of(lax.rem(b + 2 * NZ, NZ) * 48, 16), 48)

    def up_copy(k, j):
        return send(part.at[k, block(z + 8 - j)], ring_up.at[k, j], up_s.at[k, j], up_r.at[k, j], dev(dz=1))

    def dn_copy(k, j):
        return send(part.at[k, block(z - 7 + j)], ring_dn.at[k, j], dn_s.at[k, j], dn_r.at[k, j], dev(dz=-1))

    def dot(a, b):
        return jnp.dot(a, b, preferred_element_type=F32)

    ids, gates = ids_ref[...], gate_ref[...]
    e_iota = lax.broadcasted_iota(jnp.int32, (128, tok), 0)
    hot = [(ids[k : k + 1] == e_iota).astype(F32) for k in range(2)]
    sq_row = lax.broadcasted_iota(jnp.int32, (tok, tok), 0)
    sq_col = lax.broadcasted_iota(jnp.int32, (tok, tok), 1)
    before = dot((hot[0] + hot[1]).astype(BF16), (sq_row < sq_col).astype(BF16))
    r_iota = lax.broadcasted_iota(jnp.int32, (ROWS, tok), 0)
    picks = []
    for k in range(2):
        e = ids[k : k + 1]
        rank = jnp.sum(hot[k] * before, axis=0, keepdims=True).astype(jnp.int32)
        ye = (e & 3) * 2 + ((e >> 5) & 1)
        dy = (ye - y) & 7
        dx = (((e >> 3) & 3) - x) & 3
        dc = (((e >> 2) & 1) - c) & 1
        place = dy * GROUP + (dx * 2 + dc) * CAP + rank
        picks.append((r_iota == place).astype(F32))
    slot_pick[...] = (picks[0] + picks[1]).astype(BF16)
    slot_gate[...] = jnp.sum(picks[0] * gates[0:1] + picks[1] * gates[1:2], axis=1, keepdims=True)
    loads[0].wait()

    def do_send_y(k):
        cols = pl.ds(k * width, width)
        rows = (dot(slot_pick[...], grad[:, cols]) * slot_gate[...]).astype(BF16)
        y_in[k, 0:GROUP] = rows[0:GROUP]
        y_out[k, GROUP:] = rows[GROUP:]
        if k == 0:
            greet_ring()
        for d in (4, 3, 5, 2, 6, 1, 7):
            y_copy(k, d).start()

    def prepare():
        def parts_of(r):
            hi = (r * 1366) >> 16
            rest = r - hi * GROUP
            lo = (rest * 10923) >> 16
            return hi, lo, rest - lo * CAP

        def hidden_row(r):
            dxc, dy, i = parts_of(r)
            sy = (y - dy) & 7
            sx = (x - (dxc >> 1)) & 3
            sc = (c - (dxc & 1)) & 1
            return ((((sy & 1) * NX + sx) * NC + sc) * 4 + (sy >> 1)) * CAP + i

        for k, pick in enumerate((pick0, pick1)):
            pick[...] = jnp.transpose(picks[k]).astype(BF16)
            diagonal = jnp.where(sq_row == sq_col, gates[k : k + 1], 0.0)
            tok_gate[:, k : k + 1] = jnp.sum(diagonal, axis=1, keepdims=True)
        row = lax.broadcasted_iota(jnp.int32, (ROWS, 1), 0)
        col = lax.broadcasted_iota(jnp.int32, (1, ROWS), 1)
        hi, lo, i = parts_of(row)
        wide = lax.broadcasted_iota(jnp.int32, (ROWS, ROWS), 1)
        tall = lax.broadcasted_iota(jnp.int32, (ROWS, ROWS), 0)
        perm[...] = (wide == lo * GROUP + hi * CAP + i).astype(F32).astype(BF16)
        sort = (wide == hidden_row(row)).astype(F32).astype(BF16)
        unsort[...] = (tall == hidden_row(col)).astype(F32).astype(BF16)
        loads[1].wait()
        ordered = dot(sort, hid[...])
        hp[...] = ordered.astype(BF16)
        hpt[...] = jnp.transpose(ordered).astype(BF16)
        gh_acc[...] = jnp.zeros_like(gh_acc)
        loads[2].wait()

    def do_send_x(k):
        for d in range(1, NY):
            y_copy(k, d).wait_recv()
        rows = dot(perm[...], y_in[k]).astype(BF16)
        x_in[k, 0:GROUP] = rows[0:GROUP]
        x_out[k, GROUP:] = rows[GROUP:]
        for d in range(7, 0, -1):
            x_copy(k, d).start()

    def do_part(k):
        cols = pl.ds(k * width, width)
        for d in range(1, 8):
            x_copy(k, d).wait_recv()
        rows = x_in[k]
        part[k] = dot(hpt[...], rows).astype(BF16)
        up_copy(k, 0).start()
        dn_copy(k, 0).start()
        gh_acc[...] += lax.dot_general(rows, w[:, cols], (((1,), (1,)), ((), ())), preferred_element_type=F32)

    def do_ring(k, j):
        if j < 8:
            up_copy(k, j - 1).wait_recv()
            b = block(z + 8 - j)
            part[k, b] = (part[k, b].astype(F32) + ring_up[k, j - 1].astype(F32)).astype(BF16)
            up_copy(k, j).start()
            if j < 7:
                dn_copy(k, j - 1).wait_recv()
                b = block(z - 7 + j)
                part[k, b] = (part[k, b].astype(F32) + ring_dn[k, j - 1].astype(F32)).astype(BF16)
                dn_copy(k, j).start()
        else:
            up_copy(k, 7).wait_recv()
            dn_copy(k, 6).wait_recv()
            total = part[k, block(z)].astype(F32) + ring_up[k, 7].astype(F32) + ring_dn[k, 6].astype(F32)
            gd[:, pl.ds(k * width, width)] = (total * GRAD_SCALE).astype(BF16)

    def do_back_x(k):
        rows = dot(hp[...], w[:, pl.ds(k * width, width)]).astype(BF16)
        bx_in[k, 0:GROUP] = rows[0:GROUP]
        ex[k, GROUP:] = rows[GROUP:]
        for d in range(7, 0, -1):
            bx_copy(k, d).start()

    def do_back_y(k):
        for d in range(1, 8):
            bx_copy(k, d).wait_recv()
        rows = dot(perm[...], bx_in[k]).astype(BF16)
        by_in[k, 0:GROUP] = rows[0:GROUP]
        by_out[k, GROUP:] = rows[GROUP:]
        for d in (4, 3, 5, 2, 6, 1, 7):
            by_copy(k, d).start()

    def comb_store(k):
        cols = pl.ds(k * width, width)
        return pltpu.make_async_copy(comb.at[:, cols], comb_hbm.at[:, cols], out_sem.at[k])

    def do_combine(k):
        for d in range(1, NY):
            by_copy(k, d).wait_recv()
        rows = by_in[k]
        g = tok_gate[...]
        total = g[:, 0:1] * dot(pick0[...], rows) + g[:, 1:2] * dot(pick1[...], rows)
        comb[:, pl.ds(k * width, width)] = total.astype(BF16)
        comb_store(k).start()

    gh_store = pltpu.make_async_copy(gh, gh_hbm, out_sem.at[CHUNKS])
    gd_store = pltpu.make_async_copy(gd, gd_hbm, out_sem.at[CHUNKS + 1])
    prepared, joined, met_z, rings = False, False, False, 0
    for _, what, k, j in events(CHUNKS):
        if what == "send_y":
            do_send_y(k)
        else:
            if not prepared:
                prepare()
                prepared = True
            if not joined:
                greet_others(PLANE_MEMBER, 7, plane_ok)
                joined = True
            if what == "part" and not met_z:
                greet_others(Z_MEMBER, 2, z_ok)
                met_z = True
            if what == "send_x":
                do_send_x(k)
            elif what == "part":
                do_part(k)
                if k == CHUNKS - 1:
                    gh[...] = dot(unsort[...], gh_acc[...].astype(BF16)).astype(BF16)
                    gh_store.start()
            elif what == "ring":
                do_ring(k, j)
                if j == 8:
                    rings += 1
                    if rings == CHUNKS:
                        gd_store.start()
            elif what == "back_x":
                do_back_x(k)
            elif what == "back_y":
                do_back_y(k)
            else:
                do_combine(k)

    for k in range(CHUNKS):
        for d in range(1, 8):
            y_copy(k, d).wait_send()
            x_copy(k, d).wait_send()
            bx_copy(k, d).wait_send()
            by_copy(k, d).wait_send()
        for j in range(8):
            up_copy(k, j).wait_send()
        for j in range(7):
            dn_copy(k, j).wait_send()
        comb_store(k).wait()
    gh_store.wait()
    gd_store.wait()


def settle(a_ref, b_ref, c_ref, a_out, b_out, c_out, sem):
    copies = [
        pltpu.make_async_copy(src, dst, sem.at[i])
        for i, (src, dst) in enumerate(((a_ref, a_out), (b_ref, b_out), (c_ref, c_out)))
    ]
    for cp in copies:
        cp.start()
    for cp in copies:
        cp.wait()


def local(hidden, grad_output, expert_ids, gate_weights, w_down):
    rows, ff = hidden.shape
    tok, model = grad_output.shape
    width = model // CHUNKS
    any_spec = pl.BlockSpec(memory_space=pl.ANY)
    vmem_spec = pl.BlockSpec(memory_space=pltpu.VMEM)
    dma, regular = pltpu.SemaphoreType.DMA, pltpu.SemaphoreType.REGULAR
    chunked = pltpu.VMEM((CHUNKS, rows, width), BF16)
    combined, grad_hidden, grad_down = pl.pallas_call(
        kernel,
        out_shape=(
            jax.ShapeDtypeStruct((tok, model), BF16),
            jax.ShapeDtypeStruct((rows, ff), BF16),
            jax.ShapeDtypeStruct((ff // NZ, model), BF16),
        ),
        in_specs=[vmem_spec, vmem_spec, any_spec, any_spec, any_spec],
        out_specs=(any_spec, any_spec, any_spec),
        scratch_shapes=[
            pltpu.VMEM((rows, ff), BF16),
            pltpu.VMEM((tok, model), BF16),
            pltpu.VMEM((ff, model), BF16),
            pltpu.VMEM((rows, ff), BF16),
            pltpu.VMEM((ff, rows), BF16),
            pltpu.VMEM((rows, rows), BF16),
            pltpu.VMEM((rows, rows), BF16),
            pltpu.VMEM((rows, tok), BF16),
            pltpu.VMEM((tok, rows), BF16),
            pltpu.VMEM((tok, rows), BF16),
            pltpu.VMEM((rows, 1), F32),
            pltpu.VMEM((tok, 2), F32),
            chunked, chunked, chunked, chunked,
            pltpu.VMEM((CHUNKS, ff, width), BF16),
            pltpu.VMEM((CHUNKS, 8, ff // NZ, width), BF16),
            pltpu.VMEM((CHUNKS, 7, ff // NZ, width), BF16),
            chunked, chunked, chunked, chunked,
            pltpu.VMEM((rows, ff), F32),
            pltpu.VMEM((tok, model), BF16),
            pltpu.VMEM((rows, ff), BF16),
            pltpu.VMEM((ff // NZ, model), BF16),
            dma((3,)),
            dma((CHUNKS + 2,)),
            regular, regular, regular,
        ]
        + [dma((CHUNKS, 8))] * 12,
        compiler_params=pltpu.CompilerParams(
            collective_id=0, has_side_effects=True, vmem_limit_bytes=56 * 2**20
        ),
        name="moe_down",
    )(expert_ids.T, gate_weights.T, hidden, grad_output, w_down)
    combined, grad_hidden, grad_down = pl.pallas_call(
        settle,
        out_shape=(
            jax.ShapeDtypeStruct(combined.shape, BF16),
            jax.ShapeDtypeStruct(grad_hidden.shape, BF16),
            jax.ShapeDtypeStruct(grad_down.shape, BF16),
        ),
        in_specs=[any_spec] * 3,
        out_specs=(any_spec,) * 3,
        scratch_shapes=[dma((3,))],
        name="settle",
    )(combined, grad_hidden, grad_down)
    return combined, grad_hidden, grad_down[None]


def solution(mesh):
    return jax.shard_map(
        local,
        mesh=mesh,
        in_specs=(
            P(("dp", "ctx", "tp"), None),
            P(("dp", "ctx", "tp"), None),
            P(("dp", "ctx", "tp"), None),
            P(("dp", "ctx", "tp"), None),
            P(("ctx", "tp"), None, None),
        ),
        out_specs=(
            P(("dp", "ctx", "tp"), None),
            P(("dp", "ctx", "tp"), None),
            P(("ctx", "tp"), "dp", None),
        ),
        check_vma=False,
    )
```

```python
import functools

import jax
import jax.numpy as jnp
from jax import lax
from jax.experimental import pallas as pl
from jax.experimental.pallas import tpu as pltpu
from jax.sharding import PartitionSpec as P

MESH = pl.DeviceIdType.MESH
GRAD_SCALE = 0.015625
F32, BF16 = jnp.float32, jnp.bfloat16

NY, NX, NC, NZ = 8, 4, 2, 16
CAP = 6
GROUP = 8 * CAP
ROWS = 64 * CAP
HUB, PLANE_MEMBER, Z_MEMBER = 4, 0, 2
UNITS, WIDTH = 8, 256
CHUNKS = ((0, 2), (2, 2), (4, 2), (6, 1), (7, 1))
LAST = len(CHUNKS) - 1
IN_FLIGHT = 5
STRIDES = (1, 1, 1, 1, 2)
REACH = max(STRIDES)


def ring_steps(k):
    return -(-8 // STRIDES[k])


def events():
    out = []
    y_end = [13.5, 22.0, 30.6, 35.0, 39.0]
    part_at = [19.5, 28.0, 36.5, 40.0, 43.5]
    back_x_at = [6.0, 7.0, 23.5, 32.0, 42.0]
    back_y_at = [18.5, 33.0, 42.0, 50.0, 54.0]
    for k in range(len(CHUNKS)):
        out.append((0.1 * k, "send_y", k, 0))
        out.append((back_x_at[k], "back_x", k, 0))
        out.append((y_end[k], "send_x", k, 0))
        out.append((back_y_at[k], "back_y", k, 0))
        out.append((part_at[k], "part", k, 0))
        for j in range(1, ring_steps(k) + 1):
            out.append((part_at[k] + (3.0 if STRIDES[k] == 1 else 3.5) * j, "ring", k, j))
        out.append((66.0 + k, "combine", k, 0))
    return sorted(out)


def kernel(
    ids_ref, gate_ref, hid_hbm, grad_hbm, w_hbm,
    comb_hbm, gh_hbm, gd_hbm,
    hid, grad, w, hp, hpt, perm, unsort, slot_pick, pick0, pick1, slot_gate, tok_gate,
    y_out, y_in, x_out, x_in, part, ring_in,
    ex, bx_in, by_out, by_in, gh_acc, comb, gh, gd,
    in_sem, out_sem, ring_ok, plane_ok, z_ok,
    y_s, y_r, x_s, x_r, bx_s, bx_r, by_s, by_r, ring_s, ring_r,
):
    tok = grad.shape[0]
    z = lax.axis_index("dp")
    ctx = lax.axis_index("ctx")
    tp = lax.axis_index("tp")
    c = lax.rem(ctx, 2)
    x = lax.rem(ctx // 2, 4)
    y = tp * 2 + ctx // 8

    def dev(dz=0, dy=0, dx=0, dc=0):
        ny = lax.rem(y + (dy + NY), NY)
        nx = lax.rem(x + (dx + NX), NX)
        nc = lax.rem(c + (dc + NC), NC)
        nz = lax.rem(z + (dz + NZ), NZ)
        return {"dp": nz, "ctx": (lax.rem(ny, 2) * NX + nx) * NC + nc, "tp": ny // 2}

    loads = [
        pltpu.make_async_copy(grad_hbm, grad, in_sem.at[0]),
        pltpu.make_async_copy(hid_hbm, hid, in_sem.at[1]),
        pltpu.make_async_copy(w_hbm.at[0], w, in_sem.at[2]),
    ]
    loads[0].start()

    barrier = pltpu.get_barrier_semaphore()

    def tell_ring(sem):
        for d in range(1, NY):
            pl.semaphore_signal(sem, inc=1, device_id=dev(dy=d), device_id_type=MESH)

    @pl.when(y != HUB)
    def _():
        pl.semaphore_signal(barrier, inc=1, device_id=dev(dy=HUB - y + NY), device_id_type=MESH)

    def greet_ring():
        @pl.when(y == HUB)
        def _():
            pl.semaphore_wait(barrier, NY - 1)
            tell_ring(ring_ok)

        @pl.when(y != HUB)
        def _():
            pl.semaphore_wait(ring_ok, 1)

        @pl.when(y == PLANE_MEMBER)
        def _():
            for d in range(1, 8):
                pl.semaphore_signal(barrier, inc=1, device_id=dev(dx=d // 2, dc=d % 2), device_id_type=MESH)

        @pl.when(y == Z_MEMBER)
        def _():
            for d in [sign * hop for hop in range(1, REACH + 1) for sign in (1, -1)]:
                pl.semaphore_signal(barrier, inc=1, device_id=dev(dz=d), device_id_type=MESH)

    def greet_others(member, count, sem):
        @pl.when(y == member)
        def _():
            pl.semaphore_wait(barrier, count)
            tell_ring(sem)

        @pl.when(y != member)
        def _():
            pl.semaphore_wait(sem, 1)

    def send(src, dst, ssem, rsem, device):
        return pltpu.make_async_remote_copy(
            src_ref=src, dst_ref=dst, send_sem=ssem, recv_sem=rsem, device_id=device, device_id_type=MESH
        )

    def group(d):
        return pl.ds(d * GROUP, GROUP)

    def units(k):
        return pl.ds(CHUNKS[k][0], CHUNKS[k][1])

    def columns(k):
        return pl.ds(CHUNKS[k][0] * WIDTH, CHUNKS[k][1] * WIDTH)

    def each_unit(k):
        return [(u, pl.ds(u * WIDTH, WIDTH)) for u in range(CHUNKS[k][0], CHUNKS[k][0] + CHUNKS[k][1])]

    def message(out, into, sems, k, d, device):
        at = (units(k), group(d))
        return send(out.at[at], into.at[at], sems[0].at[k, d], sems[1].at[k, d], device)

    def y_copy(k, d):
        return message(y_out, y_in, (y_s, y_r), k, d, dev(dy=d))

    def x_copy(k, d):
        return message(x_out, x_in, (x_s, x_r), k, d, dev(dx=d // 2, dc=d % 2))

    def bx_copy(k, d):
        return message(ex, bx_in, (bx_s, bx_r), k, d, dev(dx=-(d // 2), dc=d % 2))

    def by_copy(k, d):
        return message(by_out, by_in, (by_s, by_r), k, d, dev(dy=-d))

    def split(rows, u, own, out):
        rows = rows.astype(BF16)
        own[u, 0:GROUP] = rows[0:GROUP]
        out[u, GROUP:] = rows[GROUP:]

    def block(b):
        return pl.ds(pl.multiple_of(lax.rem(b + 2 * NZ, NZ) * 48, 16), 48)

    def distances(k, way, j):
        far, stride = 8 if way == k % 2 else 7, STRIDES[k]
        return [d for d in range(far - stride * j, far - stride * (j + 1), -1) if d >= 1]

    def ring_block(way, d):
        return block(z + d if way == 0 else z - d)

    def ring_copy(k, way, d):
        hop = min(STRIDES[k], d)
        return send(
            part.at[units(k), ring_block(way, d)],
            ring_in.at[way, d - 1, units(k)],
            ring_s.at[way, k, d - 1],
            ring_r.at[way, k, d - 1],
            dev(dz=hop if way == 0 else -hop),
        )

    def dot(a, b):
        return jnp.dot(a, b, preferred_element_type=F32)

    ids, gates = ids_ref[...], gate_ref[...]
    e_iota = lax.broadcasted_iota(jnp.int32, (128, tok), 0)
    hot = [(ids[k : k + 1] == e_iota).astype(F32) for k in range(2)]
    sq_row = lax.broadcasted_iota(jnp.int32, (tok, tok), 0)
    sq_col = lax.broadcasted_iota(jnp.int32, (tok, tok), 1)
    before = dot((hot[0] + hot[1]).astype(BF16), (sq_row < sq_col).astype(BF16))
    r_iota = lax.broadcasted_iota(jnp.int32, (ROWS, tok), 0)
    picks = []
    for k in range(2):
        e = ids[k : k + 1]
        rank = jnp.sum(hot[k] * before, axis=0, keepdims=True).astype(jnp.int32)
        ye = (e & 3) * 2 + ((e >> 5) & 1)
        dy = (ye - y) & 7
        dx = (((e >> 3) & 3) - x) & 3
        dc = (((e >> 2) & 1) - c) & 1
        place = dy * GROUP + (dx * 2 + dc) * CAP + rank
        picks.append((r_iota == place).astype(F32))
    slot_pick[...] = (picks[0] + picks[1]).astype(BF16)
    slot_gate[...] = jnp.sum(picks[0] * gates[0:1] + picks[1] * gates[1:2], axis=1, keepdims=True)
    loads[0].wait()
    loads[1].start()
    loads[2].start()

    far_first = (4, 3, 5, 2, 6, 1, 7)

    def do_send_y(k):
        for u, cols in each_unit(k):
            split(dot(slot_pick[...], grad[:, cols]) * slot_gate[...], u, y_in, y_out)
        if k == 0:
            greet_ring()
        for d in far_first:
            y_copy(k, d).start()

    def prepare():
        def parts_of(r):
            hi = (r * 1366) >> 16
            rest = r - hi * GROUP
            lo = (rest * 10923) >> 16
            return hi, lo, rest - lo * CAP

        def hidden_row(r):
            dxc, dy, i = parts_of(r)
            sy = (y - dy) & 7
            sx = (x - (dxc >> 1)) & 3
            sc = (c - (dxc & 1)) & 1
            return ((((sy & 1) * NX + sx) * NC + sc) * 4 + (sy >> 1)) * CAP + i

        for k, pick in enumerate((pick0, pick1)):
            pick[...] = jnp.transpose(picks[k]).astype(BF16)
            diagonal = jnp.where(sq_row == sq_col, gates[k : k + 1], 0.0)
            tok_gate[:, k : k + 1] = jnp.sum(diagonal, axis=1, keepdims=True)
        row = lax.broadcasted_iota(jnp.int32, (ROWS, 1), 0)
        col = lax.broadcasted_iota(jnp.int32, (1, ROWS), 1)
        hi, lo, i = parts_of(row)
        wide = lax.broadcasted_iota(jnp.int32, (ROWS, ROWS), 1)
        tall = lax.broadcasted_iota(jnp.int32, (ROWS, ROWS), 0)
        perm[...] = (wide == lo * GROUP + hi * CAP + i).astype(F32).astype(BF16)
        sort = (wide == hidden_row(row)).astype(F32).astype(BF16)
        unsort[...] = (tall == hidden_row(col)).astype(F32).astype(BF16)
        loads[1].wait()
        ordered = dot(sort, hid[...])
        hp[...] = ordered.astype(BF16)
        hpt[...] = jnp.transpose(ordered).astype(BF16)
        gh_acc[...] = jnp.zeros_like(gh_acc)
        loads[2].wait()

    def arrived_y(k):
        for d in range(1, NY):
            y_copy(k, d).wait_recv()

    def do_send_x(k):
        for u, _ in each_unit(k):
            split(dot(perm[...], y_in[u]), u, x_in, x_out)
        for d in range(7, 0, -1):
            x_copy(k, d).start()

    def do_part(k):
        for d in range(1, 8):
            x_copy(k, d).wait_recv()
        for u, _ in each_unit(k):
            part[u] = dot(hpt[...], x_in[u]).astype(BF16)
        for way in range(2):
            for d in distances(k, way, 0):
                ring_copy(k, way, d).start()
        for u, cols in each_unit(k):
            gh_acc[...] += lax.dot_general(
                x_in[u], w[:, cols], (((1,), (1,)), ((), ())), preferred_element_type=F32
            )

    def do_ring(k, j):
        stride = STRIDES[k]
        for way in range(2):
            for d in distances(k, way, j):
                ring_copy(k, way, d + stride).wait_recv()
                at = (units(k), ring_block(way, d))
                part[at] = (part[at].astype(F32) + ring_in[way, d + stride - 1, units(k)].astype(F32)).astype(BF16)
                ring_copy(k, way, d).start()
        if j == ring_steps(k):
            ends = [(way, d) for way in range(2) for d in range(1, stride + 1)]
            for way, d in ends:
                ring_copy(k, way, d).wait_recv()
            for u, cols in each_unit(k):
                total = part[u, block(z)].astype(F32)
                for way, d in ends:
                    total += ring_in[way, d - 1, u].astype(F32)
                gd[:, cols] = (total * GRAD_SCALE).astype(BF16)

    def do_back_x(k):
        for u, cols in each_unit(k):
            split(dot(hp[...], w[:, cols]), u, bx_in, ex)
        for d in range(7, 0, -1):
            bx_copy(k, d).start()

    def do_back_y(k):
        for d in range(1, 8):
            bx_copy(k, d).wait_recv()
        for u, _ in each_unit(k):
            split(dot(perm[...], bx_in[u]), u, by_in, by_out)
        for d in far_first:
            by_copy(k, d).start()

    def comb_store(k):
        cols = columns(k)
        return pltpu.make_async_copy(comb.at[:, cols], comb_hbm.at[:, cols], out_sem.at[k])

    def arrived_back(k):
        for d in range(1, NY):
            by_copy(k, d).wait_recv()

    def do_combine(k):
        g = tok_gate[...]
        for u, cols in each_unit(k):
            total = g[:, 0:1] * dot(pick0[...], by_in[u]) + g[:, 1:2] * dot(pick1[...], by_in[u])
            comb[:, cols] = total.astype(BF16)
        comb_store(k).start()

    gh_store = pltpu.make_async_copy(gh, gh_hbm, out_sem.at[LAST + 1])
    gd_store = pltpu.make_async_copy(gd, gd_hbm, out_sem.at[LAST + 2])
    prepared, joined, met_z, rings, came, came_back = False, False, False, 0, -1, -1
    for _, what, k, j in events():
        if what == "send_y":
            if k >= IN_FLIGHT:
                came = k - IN_FLIGHT
                arrived_y(came)
            do_send_y(k)
            continue
        if not prepared:
            prepare()
            prepared = True
        if not joined:
            greet_others(PLANE_MEMBER, 7, plane_ok)
            joined = True
        if what == "part" and not met_z:
            greet_others(Z_MEMBER, 2 * REACH, z_ok)
            met_z = True
        if what == "send_x":
            if came < k:
                came = k
                arrived_y(k)
            do_send_x(k)
        elif what == "part":
            do_part(k)
            if k == LAST:
                gh[...] = dot(unsort[...], gh_acc[...].astype(BF16)).astype(BF16)
                gh_store.start()
        elif what == "ring":
            do_ring(k, j)
            if j == ring_steps(k):
                rings += 1
                if rings > LAST:
                    gd_store.start()
        elif what == "back_x":
            do_back_x(k)
        elif what == "back_y":
            do_back_y(k)
        else:
            arrived_back(k)
            do_combine(k)

    for k in range(LAST + 1):
        for d in range(1, 8):
            y_copy(k, d).wait_send()
            x_copy(k, d).wait_send()
            bx_copy(k, d).wait_send()
            by_copy(k, d).wait_send()
        for way in range(2):
            for j in range(ring_steps(k)):
                for d in distances(k, way, j):
                    ring_copy(k, way, d).wait_send()
        comb_store(k).wait()
    gh_store.wait()
    gd_store.wait()


def settle(*refs):
    for src, dst in zip(refs[:3], refs[3:]):
        dst[...] = src[...]


def local(hidden, grad_output, expert_ids, gate_weights, w_down):
    rows, ff = hidden.shape
    tok, model = grad_output.shape
    any_spec = pl.BlockSpec(memory_space=pl.ANY)
    vmem_spec = pl.BlockSpec(memory_space=pltpu.VMEM)
    dma, regular = pltpu.SemaphoreType.DMA, pltpu.SemaphoreType.REGULAR
    chunked = pltpu.VMEM((UNITS, rows, WIDTH), BF16)
    combined, grad_hidden, grad_down = pl.pallas_call(
        kernel,
        out_shape=(
            jax.ShapeDtypeStruct((tok, model), BF16),
            jax.ShapeDtypeStruct((rows, ff), BF16),
            jax.ShapeDtypeStruct((ff // NZ, model), BF16),
        ),
        in_specs=[vmem_spec, vmem_spec, any_spec, any_spec, any_spec],
        out_specs=(any_spec, any_spec, any_spec),
        scratch_shapes=[
            pltpu.VMEM((rows, ff), BF16),
            pltpu.VMEM((tok, model), BF16),
            pltpu.VMEM((ff, model), BF16),
            pltpu.VMEM((rows, ff), BF16),
            pltpu.VMEM((ff, rows), BF16),
            pltpu.VMEM((rows, rows), BF16),
            pltpu.VMEM((rows, rows), BF16),
            pltpu.VMEM((rows, tok), BF16),
            pltpu.VMEM((tok, rows), BF16),
            pltpu.VMEM((tok, rows), BF16),
            pltpu.VMEM((rows, 1), F32),
            pltpu.VMEM((tok, 2), F32),
            chunked, chunked, chunked, chunked,
            pltpu.VMEM((UNITS, ff, WIDTH), BF16),
            pltpu.VMEM((2, 8, UNITS, ff // NZ, WIDTH), BF16),
            chunked, chunked, chunked, chunked,
            pltpu.VMEM((rows, ff), F32),
            pltpu.VMEM((tok, model), BF16),
            pltpu.VMEM((rows, ff), BF16),
            pltpu.VMEM((ff // NZ, model), BF16),
            dma((3,)),
            dma((LAST + 3,)),
            regular, regular, regular,
        ]
        + [dma((LAST + 1, 8))] * 8
        + [dma((2, LAST + 1, 8))] * 2,
        compiler_params=pltpu.CompilerParams(
            collective_id=0, has_side_effects=True, vmem_limit_bytes=56 * 2**20
        ),
        name="moe_down",
    )(expert_ids.T, gate_weights.T, hidden, grad_output, w_down)
    combined, grad_hidden, grad_down = pl.pallas_call(
        settle,
        out_shape=(
            jax.ShapeDtypeStruct(combined.shape, BF16),
            jax.ShapeDtypeStruct(grad_hidden.shape, BF16),
            jax.ShapeDtypeStruct(grad_down.shape, BF16),
        ),
        in_specs=[vmem_spec] * 3,
        out_specs=(vmem_spec,) * 3,
        name="settle",
    )(combined, grad_hidden, grad_down)
    return combined, grad_hidden, grad_down[None]


def solution(mesh):
    return jax.shard_map(
        local,
        mesh=mesh,
        in_specs=(
            P(("dp", "ctx", "tp"), None),
            P(("dp", "ctx", "tp"), None),
            P(("dp", "ctx", "tp"), None),
            P(("dp", "ctx", "tp"), None),
            P(("ctx", "tp"), None, None),
        ),
        out_specs=(
            P(("dp", "ctx", "tp"), None),
            P(("dp", "ctx", "tp"), None),
            P(("ctx", "tp"), "dp", None),
        ),
        check_vma=False,
    )
```

```python
import functools

import jax
import jax.numpy as jnp
from jax import lax
from jax.experimental import pallas as pl
from jax.experimental.pallas import tpu as pltpu
from jax.sharding import PartitionSpec as P

MESH = pl.DeviceIdType.MESH
GRAD_SCALE = 0.015625
F32, BF16 = jnp.float32, jnp.bfloat16

NY, NX, NC, NZ = 8, 4, 2, 16
CAP = 6
GROUP = 8 * CAP
ROWS = 64 * CAP
HUB, PLANE_MEMBER, Z_MEMBER = 4, 0, 2
UNITS, WIDTH = 8, 256
CHUNKS = ((0, 2), (2, 2), (4, 2), (6, 1), (7, 1))
LAST = len(CHUNKS) - 1
IN_FLIGHT = 5
STRIDES = (1, 1, 1, 1, 2)
REACH = max(STRIDES)


def ring_steps(k):
    return -(-8 // STRIDES[k])


def events():
    out = []
    y_end = [7.42, 13.14, 17.44, 25.57, 30.53]
    part_at = [25.57, 28.87, 36.37, 39.58, 43.37]
    ring_at = [25.57, 30.08, 36.37, 39.58, 49.04]
    ring_step = [3.0, 3.03, 3.4, 2.99, 3.45]
    back_x_at = [3.82, 5.21, 27.02, 33.99, 42.09]
    back_y_at = [15.32, 18.17, 47.28, 49.1, 55.19]
    combine_at = [57.75, 60.52, 62.63, 70.92, 96.62]
    for k in range(len(CHUNKS)):
        out.append((0.1 * k, "send_y", k, 0))
        out.append((back_x_at[k], "back_x", k, 0))
        out.append((y_end[k], "send_x", k, 0))
        out.append((back_y_at[k], "back_y", k, 0))
        out.append((part_at[k], "part", k, 0))
        for j in range(1, ring_steps(k) + 1):
            out.append((ring_at[k] + ring_step[k] * j, "ring", k, j))
        out.append((combine_at[k], "combine", k, 0))
    return sorted(out)


def kernel(
    ids_ref, gate_ref, hid_hbm, grad_hbm, w_hbm,
    comb_hbm, gh_hbm, gd_hbm,
    hid, grad, w, hp, hpt, perm, unsort, slot_pick, pick0, pick1, slot_gate, tok_gate,
    y_out, y_in, x_out, x_in, part, ring_in,
    ex, bx_in, by_out, by_in, gh_acc, comb, gh, gd,
    in_sem, out_sem, ring_ok, plane_ok, z_ok,
    y_s, y_r, x_s, x_r, bx_s, bx_r, by_s, by_r, ring_s, ring_r,
):
    tok = grad.shape[0]
    z = lax.axis_index("dp")
    ctx = lax.axis_index("ctx")
    tp = lax.axis_index("tp")
    c = lax.rem(ctx, 2)
    x = lax.rem(ctx // 2, 4)
    y = tp * 2 + ctx // 8

    def dev(dz=0, dy=0, dx=0, dc=0):
        ny = lax.rem(y + (dy + NY), NY)
        nx = lax.rem(x + (dx + NX), NX)
        nc = lax.rem(c + (dc + NC), NC)
        nz = lax.rem(z + (dz + NZ), NZ)
        return {"dp": nz, "ctx": (lax.rem(ny, 2) * NX + nx) * NC + nc, "tp": ny // 2}

    loads = [
        pltpu.make_async_copy(grad_hbm, grad, in_sem.at[0]),
        pltpu.make_async_copy(hid_hbm, hid, in_sem.at[1]),
        pltpu.make_async_copy(w_hbm.at[0], w, in_sem.at[2]),
    ]
    loads[0].start()

    barrier = pltpu.get_barrier_semaphore()

    def tell_ring(sem):
        for d in range(1, NY):
            pl.semaphore_signal(sem, inc=1, device_id=dev(dy=d), device_id_type=MESH)

    @pl.when(y != HUB)
    def _():
        pl.semaphore_signal(barrier, inc=1, device_id=dev(dy=HUB - y + NY), device_id_type=MESH)

    def greet_ring():
        @pl.when(y == HUB)
        def _():
            pl.semaphore_wait(barrier, NY - 1)
            tell_ring(ring_ok)

        @pl.when(y != HUB)
        def _():
            pl.semaphore_wait(ring_ok, 1)

        @pl.when(y == PLANE_MEMBER)
        def _():
            for d in range(1, 8):
                pl.semaphore_signal(barrier, inc=1, device_id=dev(dx=d // 2, dc=d % 2), device_id_type=MESH)

        @pl.when(y == Z_MEMBER)
        def _():
            for d in [sign * hop for hop in range(1, REACH + 1) for sign in (1, -1)]:
                pl.semaphore_signal(barrier, inc=1, device_id=dev(dz=d), device_id_type=MESH)

    def greet_others(member, count, sem):
        @pl.when(y == member)
        def _():
            pl.semaphore_wait(barrier, count)
            tell_ring(sem)

        @pl.when(y != member)
        def _():
            pl.semaphore_wait(sem, 1)

    def send(src, dst, ssem, rsem, device):
        return pltpu.make_async_remote_copy(
            src_ref=src, dst_ref=dst, send_sem=ssem, recv_sem=rsem, device_id=device, device_id_type=MESH
        )

    def group(d):
        return pl.ds(d * GROUP, GROUP)

    def units(k):
        return pl.ds(CHUNKS[k][0], CHUNKS[k][1])

    def columns(k):
        return pl.ds(CHUNKS[k][0] * WIDTH, CHUNKS[k][1] * WIDTH)

    def each_unit(k):
        return [(u, pl.ds(u * WIDTH, WIDTH)) for u in range(CHUNKS[k][0], CHUNKS[k][0] + CHUNKS[k][1])]

    def message(out, into, sems, k, d, device):
        at = (units(k), group(d))
        return send(out.at[at], into.at[at], sems[0].at[k, d], sems[1].at[k, d], device)

    def y_copy(k, d):
        return message(y_out, y_in, (y_s, y_r), k, d, dev(dy=d))

    def x_copy(k, d):
        return message(x_out, x_in, (x_s, x_r), k, d, dev(dx=d // 2, dc=d % 2))

    def bx_copy(k, d):
        return message(ex, bx_in, (bx_s, bx_r), k, d, dev(dx=-(d // 2), dc=d % 2))

    def by_copy(k, d):
        return message(by_out, by_in, (by_s, by_r), k, d, dev(dy=-d))

    def split(rows, u, own, out):
        rows = rows.astype(BF16)
        own[u, 0:GROUP] = rows[0:GROUP]
        out[u, GROUP:] = rows[GROUP:]

    def block(b):
        return pl.ds(pl.multiple_of(lax.rem(b + 2 * NZ, NZ) * 48, 16), 48)

    def distances(k, way, j):
        far, stride = 8 if way == k % 2 else 7, STRIDES[k]
        return [d for d in range(far - stride * j, far - stride * (j + 1), -1) if d >= 1]

    def ring_block(way, d):
        return block(z + d if way == 0 else z - d)

    def ring_copy(k, way, d):
        hop = min(STRIDES[k], d)
        return send(
            part.at[units(k), ring_block(way, d)],
            ring_in.at[way, d - 1, units(k)],
            ring_s.at[way, k, d - 1],
            ring_r.at[way, k, d - 1],
            dev(dz=hop if way == 0 else -hop),
        )

    def dot(a, b):
        return jnp.dot(a, b, preferred_element_type=F32)

    ids, gates = ids_ref[...], gate_ref[...]
    e_iota = lax.broadcasted_iota(jnp.int32, (128, tok), 0)
    hot = [(ids[k : k + 1] == e_iota).astype(F32) for k in range(2)]
    sq_row = lax.broadcasted_iota(jnp.int32, (tok, tok), 0)
    sq_col = lax.broadcasted_iota(jnp.int32, (tok, tok), 1)
    before = dot((hot[0] + hot[1]).astype(BF16), (sq_row < sq_col).astype(BF16))
    r_iota = lax.broadcasted_iota(jnp.int32, (ROWS, tok), 0)
    picks = []
    for k in range(2):
        e = ids[k : k + 1]
        rank = jnp.sum(hot[k] * before, axis=0, keepdims=True).astype(jnp.int32)
        ye = (e & 3) * 2 + ((e >> 5) & 1)
        dy = (ye - y) & 7
        dx = (((e >> 3) & 3) - x) & 3
        dc = (((e >> 2) & 1) - c) & 1
        place = dy * GROUP + (dx * 2 + dc) * CAP + rank
        picks.append((r_iota == place).astype(F32))
    slot_pick[...] = (picks[0] + picks[1]).astype(BF16)
    slot_gate[...] = jnp.sum(picks[0] * gates[0:1] + picks[1] * gates[1:2], axis=1, keepdims=True)
    loads[0].wait()
    loads[1].start()
    loads[2].start()

    far_first = (4, 3, 5, 2, 6, 1, 7)

    def do_send_y(k):
        for u, cols in each_unit(k):
            split(dot(slot_pick[...], grad[:, cols]) * slot_gate[...], u, y_in, y_out)
        if k == 0:
            greet_ring()
        for d in far_first:
            y_copy(k, d).start()

    def prepare():
        def parts_of(r):
            hi = (r * 1366) >> 16
            rest = r - hi * GROUP
            lo = (rest * 10923) >> 16
            return hi, lo, rest - lo * CAP

        def hidden_row(r):
            dxc, dy, i = parts_of(r)
            sy = (y - dy) & 7
            sx = (x - (dxc >> 1)) & 3
            sc = (c - (dxc & 1)) & 1
            return ((((sy & 1) * NX + sx) * NC + sc) * 4 + (sy >> 1)) * CAP + i

        for k, pick in enumerate((pick0, pick1)):
            pick[...] = jnp.transpose(picks[k]).astype(BF16)
            diagonal = jnp.where(sq_row == sq_col, gates[k : k + 1], 0.0)
            tok_gate[:, k : k + 1] = jnp.sum(diagonal, axis=1, keepdims=True)
        row = lax.broadcasted_iota(jnp.int32, (ROWS, 1), 0)
        col = lax.broadcasted_iota(jnp.int32, (1, ROWS), 1)
        hi, lo, i = parts_of(row)
        wide = lax.broadcasted_iota(jnp.int32, (ROWS, ROWS), 1)
        tall = lax.broadcasted_iota(jnp.int32, (ROWS, ROWS), 0)
        perm[...] = (wide == lo * GROUP + hi * CAP + i).astype(F32).astype(BF16)
        sort = (wide == hidden_row(row)).astype(F32).astype(BF16)
        unsort[...] = (tall == hidden_row(col)).astype(F32).astype(BF16)
        loads[1].wait()
        ordered = dot(sort, hid[...])
        hp[...] = ordered.astype(BF16)
        hpt[...] = jnp.transpose(ordered).astype(BF16)
        gh_acc[...] = jnp.zeros_like(gh_acc)
        loads[2].wait()

    def arrived_y(k):
        for d in range(1, NY):
            y_copy(k, d).wait_recv()

    def do_send_x(k):
        for u, _ in each_unit(k):
            split(dot(perm[...], y_in[u]), u, x_in, x_out)
        for d in range(7, 0, -1):
            x_copy(k, d).start()

    def do_part(k):
        for d in range(1, 8):
            x_copy(k, d).wait_recv()
        for u, _ in each_unit(k):
            part[u] = dot(hpt[...], x_in[u]).astype(BF16)
        for way in range(2):
            for d in distances(k, way, 0):
                ring_copy(k, way, d).start()
        for u, cols in each_unit(k):
            gh_acc[...] += lax.dot_general(
                x_in[u], w[:, cols], (((1,), (1,)), ((), ())), preferred_element_type=F32
            )

    def do_ring(k, j):
        stride = STRIDES[k]
        for way in range(2):
            for d in distances(k, way, j):
                ring_copy(k, way, d + stride).wait_recv()
                at = (units(k), ring_block(way, d))
                part[at] = (part[at].astype(F32) + ring_in[way, d + stride - 1, units(k)].astype(F32)).astype(BF16)
                ring_copy(k, way, d).start()
        if j == ring_steps(k):
            ends = [(way, d) for way in range(2) for d in range(1, stride + 1)]
            for way, d in ends:
                ring_copy(k, way, d).wait_recv()
            for u, cols in each_unit(k):
                total = part[u, block(z)].astype(F32)
                for way, d in ends:
                    total += ring_in[way, d - 1, u].astype(F32)
                gd[:, cols] = (total * GRAD_SCALE).astype(BF16)

    def do_back_x(k):
        for u, cols in each_unit(k):
            split(dot(hp[...], w[:, cols]), u, bx_in, ex)
        for d in range(7, 0, -1):
            bx_copy(k, d).start()

    def do_back_y(k):
        for d in range(1, 8):
            bx_copy(k, d).wait_recv()
        for u, _ in each_unit(k):
            split(dot(perm[...], bx_in[u]), u, by_in, by_out)
        for d in far_first:
            by_copy(k, d).start()

    def comb_store(k):
        cols = columns(k)
        return pltpu.make_async_copy(comb.at[:, cols], comb_hbm.at[:, cols], out_sem.at[k])

    def arrived_back(k):
        for d in range(1, NY):
            by_copy(k, d).wait_recv()

    def do_combine(k):
        g = tok_gate[...]
        for u, cols in each_unit(k):
            total = g[:, 0:1] * dot(pick0[...], by_in[u]) + g[:, 1:2] * dot(pick1[...], by_in[u])
            comb[:, cols] = total.astype(BF16)
        comb_store(k).start()

    gh_store = pltpu.make_async_copy(gh, gh_hbm, out_sem.at[LAST + 1])
    gd_store = pltpu.make_async_copy(gd, gd_hbm, out_sem.at[LAST + 2])
    prepared, joined, met_z, rings, came, came_back = False, False, False, 0, -1, -1
    for _, what, k, j in events():
        if what == "send_y":
            if k >= IN_FLIGHT:
                came = k - IN_FLIGHT
                arrived_y(came)
            do_send_y(k)
            continue
        if not prepared:
            prepare()
            prepared = True
        if not joined:
            greet_others(PLANE_MEMBER, 7, plane_ok)
            joined = True
        if what == "part" and not met_z:
            greet_others(Z_MEMBER, 2 * REACH, z_ok)
            met_z = True
        if what == "send_x":
            if came < k:
                came = k
                arrived_y(k)
            do_send_x(k)
        elif what == "part":
            do_part(k)
            if k == LAST:
                gh[...] = dot(unsort[...], gh_acc[...].astype(BF16)).astype(BF16)
                gh_store.start()
        elif what == "ring":
            do_ring(k, j)
            if j == ring_steps(k):
                rings += 1
                if rings > LAST:
                    gd_store.start()
        elif what == "back_x":
            do_back_x(k)
        elif what == "back_y":
            do_back_y(k)
        else:
            arrived_back(k)
            do_combine(k)

    for k in range(LAST + 1):
        for d in range(1, 8):
            y_copy(k, d).wait_send()
            x_copy(k, d).wait_send()
            bx_copy(k, d).wait_send()
            by_copy(k, d).wait_send()
        for way in range(2):
            for j in range(ring_steps(k)):
                for d in distances(k, way, j):
                    ring_copy(k, way, d).wait_send()
        comb_store(k).wait()
    gh_store.wait()
    gd_store.wait()


def settle(*refs):
    for src, dst in zip(refs[:3], refs[3:]):
        dst[...] = src[...]


def local(hidden, grad_output, expert_ids, gate_weights, w_down):
    rows, ff = hidden.shape
    tok, model = grad_output.shape
    any_spec = pl.BlockSpec(memory_space=pl.ANY)
    vmem_spec = pl.BlockSpec(memory_space=pltpu.VMEM)
    dma, regular = pltpu.SemaphoreType.DMA, pltpu.SemaphoreType.REGULAR
    chunked = pltpu.VMEM((UNITS, rows, WIDTH), BF16)
    combined, grad_hidden, grad_down = pl.pallas_call(
        kernel,
        out_shape=(
            jax.ShapeDtypeStruct((tok, model), BF16),
            jax.ShapeDtypeStruct((rows, ff), BF16),
            jax.ShapeDtypeStruct((ff // NZ, model), BF16),
        ),
        in_specs=[vmem_spec, vmem_spec, any_spec, any_spec, any_spec],
        out_specs=(any_spec, any_spec, any_spec),
        scratch_shapes=[
            pltpu.VMEM((rows, ff), BF16),
            pltpu.VMEM((tok, model), BF16),
            pltpu.VMEM((ff, model), BF16),
            pltpu.VMEM((rows, ff), BF16),
            pltpu.VMEM((ff, rows), BF16),
            pltpu.VMEM((rows, rows), BF16),
            pltpu.VMEM((rows, rows), BF16),
            pltpu.VMEM((rows, tok), BF16),
            pltpu.VMEM((tok, rows), BF16),
            pltpu.VMEM((tok, rows), BF16),
            pltpu.VMEM((rows, 1), F32),
            pltpu.VMEM((tok, 2), F32),
            chunked, chunked, chunked, chunked,
            pltpu.VMEM((UNITS, ff, WIDTH), BF16),
            pltpu.VMEM((2, 8, UNITS, ff // NZ, WIDTH), BF16),
            chunked, chunked, chunked, chunked,
            pltpu.VMEM((rows, ff), F32),
            pltpu.VMEM((tok, model), BF16),
            pltpu.VMEM((rows, ff), BF16),
            pltpu.VMEM((ff // NZ, model), BF16),
            dma((3,)),
            dma((LAST + 3,)),
            regular, regular, regular,
        ]
        + [dma((LAST + 1, 8))] * 8
        + [dma((2, LAST + 1, 8))] * 2,
        compiler_params=pltpu.CompilerParams(
            collective_id=0, has_side_effects=True, vmem_limit_bytes=56 * 2**20
        ),
        name="moe_down",
    )(expert_ids.T, gate_weights.T, hidden, grad_output, w_down)
    combined, grad_hidden, grad_down = pl.pallas_call(
        settle,
        out_shape=(
            jax.ShapeDtypeStruct(combined.shape, BF16),
            jax.ShapeDtypeStruct(grad_hidden.shape, BF16),
            jax.ShapeDtypeStruct(grad_down.shape, BF16),
        ),
        in_specs=[vmem_spec] * 3,
        out_specs=(vmem_spec,) * 3,
        name="settle",
    )(combined, grad_hidden, grad_down)
    return combined, grad_hidden, grad_down[None]


def solution(mesh):
    return jax.shard_map(
        local,
        mesh=mesh,
        in_specs=(
            P(("dp", "ctx", "tp"), None),
            P(("dp", "ctx", "tp"), None),
            P(("dp", "ctx", "tp"), None),
            P(("dp", "ctx", "tp"), None),
            P(("ctx", "tp"), None, None),
        ),
        out_specs=(
            P(("dp", "ctx", "tp"), None),
            P(("dp", "ctx", "tp"), None),
            P(("ctx", "tp"), "dp", None),
        ),
        check_vma=False,
    )
```
